32 devices in a mesh: aux: 16 (over z, x, core), pair: 2 (over y).
Axes of the slice: x: 2, y: 2, z: 4, core: 2. Of those that a mesh axis runs over, the one named last changes fastest.
Arguments:
- blocks: bfloat16 [16, 2, 32, 128, 128], P('aux', 'pair'), may hold values from -6 to 6
- block_list: int32 [16, 2, 32, 3], P('aux', 'pair'), may hold values from -1 to 79, as said below
- metric: bfloat16 [4096, 256], P('aux'), may hold values from -0.1875 to 0.1875
- virt_energy: float32 [20480], replicated, may hold values from 0.2 to 3
- occ_energy: float32 [8000], replicated, may hold values from -2 to -0.5
- pair_list: int32 [1, 2], replicated, may hold values from 0 to 7999
Outputs:
- amplitudes: bfloat16 [2, 16, 10240], P('pair', None, 'aux')
- density: float32 [8, 8], replicated
The draws below stay inside these ranges and needn't reach their ends.
Inputs may be any that keep to these rules, and one draw needn't show every extreme that they name: `block_list`: each entry is (occupied slot, virtual block, auxiliary block). Live entries have slot 0 or 1 (the pair's first or second orbital), virtual block 0 to 79 within the device's virtual half, auxiliary block 0 or 1; padding entries have slot -1 and stand anywhere in the list; no live triple repeats within one device's list; in every draw some device has all 32 entries live and some device has padding.
All inputs are finite; a program needn't handle non-finite values.
Results may differ from the reference program's by a relative error of at most 0.0049.
Values may be sent and summed in bfloat16 or wider, within the bound.
A program may use at most 128 MiB of HBM per device.

```python
import math
import jax
import jax.numpy as jnp
from jax import lax

V = 20480
NOCC = 8000
AUX_DEV = 256
VB = 128
NBLK = 32
NAUX = 4096
PBK = 128
NVB = 80
HALF = 8
PAIRS = 1
N_AUX = 16
N_PAIR = 2


def draw_block_list(key, part):
    key = jax.random.fold_in(key, 11)
    device_count = N_AUX * N_PAIR
    slot_total = 4 * NVB
    keys = jax.random.split(key, 3)
    live_count = jax.random.randint(keys[0], (device_count,), NBLK // 3, NBLK)
    full_device = jax.random.randint(keys[1], (), 0, device_count)
    live_count = jnp.where(jnp.arange(device_count) == full_device, NBLK, live_count)

    def one_device(device_key, count):
        pick_key, rank_key = jax.random.split(device_key)
        chosen = jax.random.permutation(pick_key, slot_total)[:NBLK]
        ranking = jax.random.permutation(rank_key, NBLK)
        live = ranking < count
        occ_slot = chosen // (2 * NVB)
        remainder = chosen % (2 * NVB)
        vblock = remainder // 2
        aux_block = remainder % 2
        occ_slot = jnp.where(live, occ_slot, -1)
        return jnp.stack([occ_slot, vblock, aux_block], axis=-1).astype(jnp.int32)
    device_keys = jax.random.split(keys[2], device_count)
    table = jax.vmap(one_device)(device_keys, live_count)
    return table.reshape(N_AUX, N_PAIR, NBLK, 3)


def steps_of(stream_key, extent, cuts, smallest, top_value):
    def one(axis_at, blocks):
        steps = jax.random.uniform(jax.random.fold_in(jax.random.fold_in(stream_key, 6), axis_at), (blocks,), jnp.float32, smallest / len(cuts), top_value / len(cuts))
        return jnp.repeat(jnp.exp(steps), extent[axis_at] // blocks).reshape((-1,) + (1,) * (len(extent) - axis_at - 1))

    loudness = one(*cuts[0])
    for cut in cuts[1:]:
        loudness = loudness * one(*cut)
    return loudness


def gaussian(rng, dims, scale, most, cuts=(), held_as=jnp.bfloat16):
    values = scale * jax.random.normal(rng, dims, jnp.float32)
    if cuts:
        values = values * steps_of(rng, dims, cuts, -0.22, 0.18)
    return jnp.clip(values, -most, most).astype(held_as)


def setup_inputs(seed: int = 0) -> dict:
    splits = jax.random.split(jax.random.key(seed), 7)
    blocks = gaussian(splits[0], (N_AUX, N_PAIR, NBLK, VB, PBK), 1.0, 6.0, ((0, 16), (1, 2)))
    block_list = draw_block_list(jax.random.fold_in(splits[6], 71), 0)
    metric = gaussian(splits[2], (NAUX, AUX_DEV), (NAUX // 4) ** -0.5, 0.1875, ((0, 16),))
    virt_energy = jnp.clip(jax.random.uniform(splits[3], (V,), jnp.float32, 0.2, 3.0), 0.2, 3.0)
    occ_energy = jnp.clip(jax.random.uniform(splits[4], (NOCC,), jnp.float32, -2.0, -0.5), -2.0, -0.5)
    pair_list = jax.random.randint(splits[5], (PAIRS, 2), 0, NOCC).astype(jnp.int32)
    return {"blocks": blocks, "block_list": block_list, "metric": metric, "virt_energy": virt_energy, "occ_energy": occ_energy, "pair_list": pair_list}


def build_shard(operands):
    raw_blocks, entries, factor = operands
    half_width = V // 2
    vblock_count = half_width // VB
    block_aux = AUX_DEV // 2
    factor_pair = factor.reshape(2, block_aux, AUX_DEV).astype(jnp.float32)
    picked = jnp.where((entries[:, 2] == 0)[:, None, None], factor_pair[0][None], factor_pair[1][None])
    terms = jnp.einsum('evk,ekn->evn', raw_blocks.astype(jnp.float32), picked)
    slot_index = jnp.where(entries[:, 0] >= 0, entries[:, 0] * vblock_count + entries[:, 1], 2 * vblock_count)
    summed = jax.ops.segment_sum(terms, slot_index.astype(jnp.int32), num_segments=2 * vblock_count)
    return summed.astype(jnp.bfloat16).reshape(2, half_width, AUX_DEV)

def reference(blocks, block_list, metric, virt_energy, occ_energy, pair_list):
    half_width = V // 2
    factors = metric.reshape(N_AUX, AUX_DEV, AUX_DEV)
    density = jnp.zeros((HALF, HALF), jnp.float32)
    window_energy = jnp.concatenate([virt_energy[:HALF], virt_energy[half_width:half_width + HALF]])
    amp_rows = []
    for pair_index in range(PAIRS):
        halves = []
        for half_index in range(2):
            column = 2 * pair_index + half_index
            shards = lax.map(build_shard, (blocks[:, column], block_list[:, column], factors))
            halves.append(jnp.transpose(shards, (1, 2, 0, 3)).reshape(2, half_width, NAUX))
        orbitals = jnp.concatenate(halves, axis=1)
        window = jnp.concatenate([orbitals[:, :HALF], orbitals[:, half_width:half_width + HALF]], axis=1)
        first_orb = pair_list[pair_index, 0]
        second_orb = pair_list[pair_index, 1]
        coulomb_u = jnp.dot(window[0], orbitals[1].T, preferred_element_type=jnp.float32)
        coulomb_r = jnp.dot(window[1], orbitals[0].T, preferred_element_type=jnp.float32)
        denominator = window_energy[:, None] + virt_energy[None, :] - occ_energy[first_orb] - occ_energy[second_orb]
        amp_u = (coulomb_u / denominator).astype(jnp.bfloat16)
        amp_r = (coulomb_r / denominator).astype(jnp.bfloat16)
        left_rows = jnp.concatenate([amp_u[:HALF], amp_r[:HALF]], axis=0)
        right_rows = jnp.concatenate([amp_u[HALF:], amp_r[HALF:]], axis=0)
        gram = jnp.dot(left_rows, right_rows.T, preferred_element_type=jnp.float32)
        density = density + 2.0 * (gram[:HALF, :HALF] + gram[HALF:, HALF:]) - gram[HALF:, :HALF] - gram[:HALF, HALF:]
        amp_rows.append(amp_u[:, :half_width])
        amp_rows.append(amp_u[:, half_width:])
    return (jnp.stack(amp_rows), density / math.sqrt(V))
```

```python
import functools
import math

import jax
import jax.numpy as jnp
from jax import lax
from jax.experimental import pallas as pl
from jax.experimental.pallas import tpu as pltpu
from jax.sharding import PartitionSpec as P

V = 20480
HALF = 8
MESH = pl.DeviceIdType.MESH
F32 = jnp.float32
BF16 = jnp.bfloat16


def table_kernel(nvb, list_ref, occ_ref, pair_ref, tab_ref, eps_ref, inv_ref):
    count = list_ref.shape[0]
    slots = 2 * nvb

    def clear(i, _):
        tab_ref[i] = count
        inv_ref[2 * i] = count
        inv_ref[2 * i + 1] = count
        return 0

    lax.fori_loop(0, slots, clear, 0, unroll=8)

    def place(e, _):
        o = list_ref[e, 0]
        v = list_ref[e, 1]
        k = list_ref[e, 2]

        @pl.when(o >= 0)
        def _():
            inv_ref[2 * (o * nvb + v) + k] = e
            tab_ref[(1 - o) * nvb + v] = e

        return 0

    lax.fori_loop(0, count, place, 0)

    def partners(e, _):
        o = list_ref[e, 0]
        v = list_ref[e, 1]
        live = o >= 0
        at = jnp.where(live, 2 * (o * nvb + v), 0)
        tab_ref[slots + e] = jnp.where(live, inv_ref[at], count)
        tab_ref[slots + count + e] = jnp.where(live, inv_ref[at + 1], count)
        return 0

    lax.fori_loop(0, count, partners, 0)
    for o in range(2):
        for k in range(2):
            tab_ref[slots + 2 * count + 2 * o + k] = inv_ref[2 * o * nvb + k]
    q = lax.axis_index("pair") // 2
    eps_ref[0] = occ_ref[pair_ref[q, 0]]
    eps_ref[1] = occ_ref[pair_ref[q, 1]]


def main_kernel(
    n_aux, n_pair, nvb, slab, nb,
    tab_ref, eps_ref, blocks_ref, metric_ref, ven_ref,
    amp_ref, den_ref,
    held, three, part, wsend, wrecv, csend, crecv, dsend, drecv, psum_buf, asum_buf,
    load_sem, w_sems, cs_sems, cr_sems, ds_sems, dr_sems, ps_sems, pr_sems, as_sems, ar_sems,
):
    count = blocks_ref.shape[0]
    lanes = blocks_ref.shape[1]
    slots = 2 * nvb
    n_t = n_aux // 2
    me = lax.axis_index("aux")
    p = lax.axis_index("pair")
    core = me % 2
    my_t = me // 2
    half = p % 2
    mate = p + 1 - 2 * half
    other = me + 1 - 2 * core

    load = pltpu.make_async_copy(blocks_ref, held.at[pl.ds(0, count)], load_sem)
    load.start()

    psum_buf[...] = jnp.zeros_like(psum_buf)
    barrier = pltpu.get_barrier_semaphore()

    def greet_aux(s, _):
        pl.semaphore_signal(barrier, inc=1, device_id=((me + s) % n_aux, p), device_id_type=MESH)
        return 0

    def greet_pair(s, _):
        pl.semaphore_signal(barrier, inc=1, device_id=(me, (p + s) % n_pair), device_id_type=MESH)
        return 0

    lax.fori_loop(1, n_pair, greet_pair, 0)
    lax.fori_loop(1, n_aux, greet_aux, 0)

    held[count] = jnp.zeros(held.shape[1:], BF16)
    part[count] = jnp.zeros(part.shape[1:], F32)
    load.wait()
    own = [
        held[tab_ref[slots + 2 * count + i], :16, :].astype(F32)[:HALF] for i in range(4)
    ]
    wsend[...] = jnp.concatenate(own, axis=0).astype(BF16)
    pl.semaphore_wait(barrier, n_aux + n_pair - 2)
    wcopy = pltpu.make_async_remote_copy(
        src_ref=wsend, dst_ref=wrecv, send_sem=w_sems.at[0], recv_sem=w_sems.at[1],
        device_id=(me, mate), device_id_type=MESH,
    )
    wcopy.start()

    metric = metric_ref[...]

    def transform(e, _):
        rows = jnp.concatenate(
            [held[tab_ref[slots + e]], held[tab_ref[slots + count + e]]], axis=1
        )
        three[e] = jnp.dot(rows, metric, preferred_element_type=F32).astype(BF16)
        return 0

    lax.fori_loop(0, count, transform, 0, unroll=4)

    wcopy.wait()
    theirs = wrecv[...].astype(F32)
    rows = []
    for o in range(2):
        mine = jnp.concatenate([own[2 * o], own[2 * o + 1]], axis=1)
        got = jnp.concatenate(
            [theirs[16 * o : 16 * o + HALF], theirs[16 * o + HALF : 16 * o + 16]], axis=1
        )
        rows.append(jnp.where(half == 0, mine, got))
        rows.append(jnp.where(half == 0, got, mine))
    window = jnp.dot(
        jnp.concatenate(rows, axis=0).astype(BF16), metric, preferred_element_type=F32
    ).astype(BF16)

    def contract(e, _):
        part[e] = lax.dot_general(
            window, three[e], (((1,), (1,)), ((), ())), preferred_element_type=F32
        )
        return 0

    lax.fori_loop(0, count, contract, 0, unroll=4)

    def first_block(d):
        return (d * slab) // lanes

    def piece(d, c, j):
        return part[tab_ref[c * nvb + first_block(d) + j], 16 * c : 16 * (c + 1), :]

    def c_copy(t):
        return pltpu.make_async_remote_copy(
            src_ref=csend.at[t], dst_ref=crecv.at[t],
            send_sem=cs_sems.at[t], recv_sem=cr_sems.at[t],
            device_id=(other, p), device_id_type=MESH,
        )

    def d_copy(t, slot):
        return pltpu.make_async_remote_copy(
            src_ref=dsend.at[t], dst_ref=drecv.at[slot],
            send_sem=ds_sems.at[t], recv_sem=dr_sems.at[slot],
            device_id=(2 * t + core, p), device_id_type=MESH,
        )

    def to_core(s, _):
        t = (my_t + s) % n_t
        d = 2 * t + 1 - core
        for c in range(2):
            for j in range(nb):
                csend[t, 16 * c : 16 * (c + 1), lanes * j : lanes * (j + 1)] = piece(d, c, j)
        c_copy(t).start()
        return 0

    lax.fori_loop(1, n_t + 1, to_core, 0)

    def to_chip(s, _):
        t = (my_t + s) % n_t
        d = 2 * t + core
        c_copy(t).wait_recv()
        for c in range(2):
            for j in range(nb):
                here = (slice(16 * c, 16 * (c + 1)), slice(lanes * j, lanes * (j + 1)))
                dsend[(t,) + here] = (piece(d, c, j) + crecv[(t,) + here]).astype(BF16)
        d_copy(t, my_t).start()
        return 0

    lax.fori_loop(1, n_t, to_chip, 0)
    c_copy(my_t).wait_recv()

    first = first_block(me)
    offset = me * slab - first * lanes
    sub = lax.broadcasted_iota(jnp.int32, (16, lanes), 0)
    lane = lax.broadcasted_iota(jnp.int32, (16, lanes), 1)
    tops = jnp.where(sub < HALF, ven_ref[0:1, :], ven_ref[nvb : nvb + 1, :])
    column = jnp.sum(jnp.where(lane == sub % HALF, tops, 0.0), axis=1, keepdims=True)

    totals = []
    for c in range(2):
        for j in range(nb):
            here = (slice(16 * c, 16 * (c + 1)), slice(lanes * j, lanes * (j + 1)))
            totals.append(piece(me, c, j) + crecv[(my_t,) + here])

    def arrive(s, totals):
        t = (my_t + n_t - s) % n_t
        pltpu.make_async_remote_copy(
            src_ref=dsend.at[t], dst_ref=drecv.at[t],
            send_sem=ds_sems.at[t], recv_sem=dr_sems.at[t],
            device_id=(2 * t + core, p), device_id_type=MESH,
        ).wait_recv()
        out = []
        for c in range(2):
            for j in range(nb):
                here = (slice(16 * c, 16 * (c + 1)), slice(lanes * j, lanes * (j + 1)))
                out.append(totals[c * nb + j] + drecv[(t,) + here].astype(F32))
        return tuple(out)

    totals = lax.fori_loop(1, n_t, arrive, tuple(totals))

    grams = [[jnp.zeros((HALF, HALF), F32) for _ in range(2)] for _ in range(2)]
    for j in range(nb):
        energy = ven_ref[pl.ds(half * nvb + first + j, 1), :]
        denominator = column + energy - eps_ref[0] - eps_ref[1]
        heads, tails = [], []
        for c in range(2):
            scaled = (totals[c * nb + j] / denominator).astype(BF16)
            if c == 0:
                amp_ref[:, lanes * j : lanes * (j + 1)] = scaled
            wide = scaled.astype(F32)
            if slab % lanes:
                at = lane + (j * lanes - offset)
                wide = jnp.where(jnp.logical_and(at >= 0, at < slab), wide, 0.0)
            heads.append(wide[:HALF].astype(BF16))
            tails.append(wide[HALF:].astype(BF16))
        for a in range(2):
            for b in range(2):
                grams[a][b] += lax.dot_general(
                    heads[a], tails[b], (((1,), (1,)), ((), ())), preferred_element_type=F32
                )
    psum_buf[p, :, :HALF] = (
        2.0 * (grams[0][0] + grams[1][1]) - grams[1][0] - grams[0][1]
    )

    def p_copy(q, slot):
        return pltpu.make_async_remote_copy(
            src_ref=psum_buf.at[p], dst_ref=psum_buf.at[slot],
            send_sem=ps_sems.at[q], recv_sem=pr_sems.at[slot],
            device_id=(me, q), device_id_type=MESH,
        )

    def p_send(s, _):
        p_copy((p + s) % n_pair, p).start()
        return 0

    lax.fori_loop(1, n_pair, p_send, 0)

    def p_wait(s, _):
        q = (p + s) % n_pair
        p_copy(q, q).wait()
        return 0

    lax.fori_loop(1, n_pair, p_wait, 0)
    total = psum_buf[0]
    for q in range(1, n_pair):
        total = total + psum_buf[q]
    asum_buf[me] = total

    def a_copy(d, slot):
        return pltpu.make_async_remote_copy(
            src_ref=asum_buf.at[me], dst_ref=asum_buf.at[slot],
            send_sem=as_sems.at[d], recv_sem=ar_sems.at[slot],
            device_id=(d, p), device_id_type=MESH,
        )

    def a_send(s, _):
        a_copy((me + s) % n_aux, me).start()
        return 0

    lax.fori_loop(1, n_aux, a_send, 0)

    def sent(s, _):
        t = (my_t + s) % n_t
        d_copy(t, my_t).wait_send()
        c_copy(t).wait_send()
        return 0

    lax.fori_loop(1, n_t, sent, 0)
    c_copy(my_t).wait_send()

    def a_wait(s, _):
        d = (me + s) % n_aux
        a_copy(d, d).wait()
        return 0

    lax.fori_loop(1, n_aux, a_wait, 0)
    total = asum_buf[0]
    for d in range(1, n_aux):
        total = total + asum_buf[d]
    den_ref[...] = (total / math.sqrt(V))[:, :HALF]


def body(blocks, block_list, metric, virt_energy, occ_energy, pair_list):
    n_aux = lax.axis_size("aux")
    n_pair = lax.axis_size("pair")
    raw = blocks[0, 0]
    entries = block_list[0, 0]
    count, lanes = raw.shape[0], raw.shape[1]
    width = virt_energy.shape[0] // 2
    nvb = width // lanes
    slab = width // n_aux
    nb = max(-(-((d + 1) * slab) // lanes) - d * slab // lanes for d in range(n_aux))
    shard = metric.shape[1]
    n_t = n_aux // 2
    vmem = pl.BlockSpec(memory_space=pltpu.VMEM)
    smem = pl.BlockSpec(memory_space=pltpu.SMEM)
    table, eps = pl.pallas_call(
        functools.partial(table_kernel, nvb),
        out_shape=(
            jax.ShapeDtypeStruct((2 * nvb + 2 * count + 4,), jnp.int32),
            jax.ShapeDtypeStruct((2,), F32),
        ),
        in_specs=[smem] * 3,
        out_specs=(smem, smem),
        scratch_shapes=[pltpu.SMEM((4 * nvb,), jnp.int32)],
        name="tables",
    )(entries, occ_energy, pair_list)
    dma = pltpu.SemaphoreType.DMA
    amp, density = pl.pallas_call(
        functools.partial(main_kernel, n_aux, n_pair, nvb, slab, nb),
        out_shape=(
            jax.ShapeDtypeStruct((2 * HALF, nb * lanes), BF16),
            jax.ShapeDtypeStruct((HALF, HALF), F32),
        ),
        in_specs=[smem, smem, pl.BlockSpec(memory_space=pl.ANY), vmem, vmem],
        out_specs=(vmem, vmem),
        scratch_shapes=[
            pltpu.VMEM((count + 1, lanes, raw.shape[2]), BF16),
            pltpu.VMEM((count, lanes, shard), BF16),
            pltpu.VMEM((count + 1, 32, lanes), F32),
            pltpu.VMEM((32, lanes), BF16),
            pltpu.VMEM((32, lanes), BF16),
            pltpu.VMEM((n_t, 32, nb * lanes), F32),
            pltpu.VMEM((n_t, 32, nb * lanes), F32),
            pltpu.VMEM((n_t, 32, nb * lanes), BF16),
            pltpu.VMEM((n_t, 32, nb * lanes), BF16),
            pltpu.VMEM((n_pair, HALF, lanes), F32),
            pltpu.VMEM((n_aux, HALF, lanes), F32),
            dma,
            dma((2,)),
            dma((n_t,)),
            dma((n_t,)),
            dma((n_t,)),
            dma((n_t,)),
            dma((n_pair,)),
            dma((n_pair,)),
            dma((n_aux,)),
            dma((n_aux,)),
        ],
        compiler_params=pltpu.CompilerParams(
            collective_id=0, has_side_effects=True, vmem_limit_bytes=40 * 2**20
        ),
        name="amplitudes",
    )(table, eps, raw, metric, virt_energy.reshape(-1, lanes))
    if slab % lanes:
        me = lax.axis_index("aux")
        amp = lax.dynamic_slice_in_dim(amp, me * slab - me * slab // lanes * lanes, slab, 1)
    return (amp[None], density)


def solution(mesh):
    in_specs = (
        P("aux", "pair", None, None, None),
        P("aux", "pair", None, None),
        P("aux", None),
        P(),
        P(),
        P(),
    )
    out_specs = (P("pair", None, "aux"), P())
    return jax.shard_map(body, mesh=mesh, in_specs=in_specs, out_specs=out_specs, check_vma=False)
```

```python
import functools
import math

import jax
import jax.numpy as jnp
from jax import lax
from jax.experimental import pallas as pl
from jax.experimental.pallas import tpu as pltpu
from jax.sharding import PartitionSpec as P

V = 20480
HALF = 8
MESH = pl.DeviceIdType.MESH
F32 = jnp.float32
BF16 = jnp.bfloat16


def index_table(nvb, count, list_ref):
    row = lax.broadcasted_iota(jnp.int32, (8, 128), 0)
    lane = lax.broadcasted_iota(jnp.int32, (8, 128), 1)

    def slot_of(e):
        o = list_ref[0, 0, e]
        return jnp.where(o >= 0, o * nvb + list_ref[1, 0, e], -1)

    def spread(e, slots):
        return jnp.where(lane == e, slot_of(e), slots)

    slots = lax.fori_loop(0, count, spread, jnp.full((8, 128), -2, jnp.int32), unroll=8)
    slots = jnp.where(slots < 0, -2, slots)
    by_block = jnp.where(lane < nvb, jnp.where(row == 0, nvb + lane, lane), -2)
    by_window = jnp.where(lane < 4, jnp.where(lane < 2, 0, nvb), -2)
    key = jnp.where(row < 2, by_block, jnp.where(row < 4, slots, by_window))
    aux = jnp.where(row < 2, -1, jnp.where(row < 4, row - 2, jnp.bitwise_and(lane, 1)))

    def enter(e, table):
        hit = (key == slot_of(e)) & ((aux < 0) | (aux == list_ref[2, 0, e]))
        return jnp.where(hit, e, table)

    return lax.fori_loop(0, count, enter, jnp.full((8, 128), count, jnp.int32), unroll=8)


def main_kernel(
    n_aux, n_pair, nvb, slab, nb,
    list_hbm, occ_hbm, pair_hbm, blocks_ref, metric_hbm, ven_hbm,
    amp_ref, den_ref,
    list_ref, occ_ref, pair_ref, metric_ref, ven_ref, tab_vmem, tab_ref,
    held, three, part, wsend, wrecv, csend, crecv, dsend, drecv, psum_buf, asum_buf,
    load_sems, w_sems, cs_sems, cr_sems, ds_sems, dr_sems, ps_sems, pr_sems, as_sems, ar_sems,
):
    count = blocks_ref.shape[0]
    lanes = blocks_ref.shape[1]
    n_t = n_aux // 2
    me = lax.axis_index("aux")
    p = lax.axis_index("pair")
    core = me % 2
    my_t = me // 2
    half = p % 2
    mate = p + 1 - 2 * half
    other = me + 1 - 2 * core

    loads = [
        pltpu.make_async_copy(src, dst, load_sems.at[i])
        for i, (src, dst) in enumerate([
            (list_hbm, list_ref),
            (blocks_ref, held.at[pl.ds(0, count)]),
            (metric_hbm, metric_ref),
            (pair_hbm, pair_ref),
            (occ_hbm, occ_ref),
            (ven_hbm, ven_ref),
        ])
    ]
    for load in loads:
        load.start()

    psum_buf[...] = jnp.zeros_like(psum_buf)
    barrier = pltpu.get_barrier_semaphore()

    def greet_aux(s, _):
        pl.semaphore_signal(barrier, inc=1, device_id=((me + s) % n_aux, p), device_id_type=MESH)
        return 0

    def greet_pair(s, _):
        pl.semaphore_signal(barrier, inc=1, device_id=(me, (p + s) % n_pair), device_id_type=MESH)
        return 0

    lax.fori_loop(1, n_pair, greet_pair, 0)
    lax.fori_loop(1, n_aux, greet_aux, 0)

    held[count] = jnp.zeros(held.shape[1:], BF16)
    part[count] = jnp.zeros(part.shape[1:], F32)
    loads[0].wait()
    tab_vmem[...] = index_table(nvb, count, list_ref)
    fill = pltpu.make_async_copy(tab_vmem, tab_ref, load_sems.at[len(loads)])
    fill.start()
    loads[1].wait()
    fill.wait()
    own = [held[tab_ref[4, i], :16, :].astype(F32)[:HALF] for i in range(4)]
    wsend[...] = jnp.concatenate(own, axis=0).astype(BF16)
    pl.semaphore_wait(barrier, n_aux + n_pair - 2)
    wcopy = pltpu.make_async_remote_copy(
        src_ref=wsend, dst_ref=wrecv, send_sem=w_sems.at[0], recv_sem=w_sems.at[1],
        device_id=(me, mate), device_id_type=MESH,
    )
    wcopy.start()

    loads[2].wait()
    metric = metric_ref[...]

    def transform(e, _):
        rows = jnp.concatenate(
            [held[tab_ref[2, e]], held[tab_ref[3, e]]], axis=1
        )
        three[e] = jnp.dot(rows, metric, preferred_element_type=F32).astype(BF16)
        return 0

    lax.fori_loop(0, count, transform, 0, unroll=4)

    wcopy.wait()
    theirs = wrecv[...].astype(F32)
    rows = []
    for o in range(2):
        mine = jnp.concatenate([own[2 * o], own[2 * o + 1]], axis=1)
        got = jnp.concatenate(
            [theirs[16 * o : 16 * o + HALF], theirs[16 * o + HALF : 16 * o + 16]], axis=1
        )
        rows.append(jnp.where(half == 0, mine, got))
        rows.append(jnp.where(half == 0, got, mine))
    window = jnp.dot(
        jnp.concatenate(rows, axis=0).astype(BF16), metric, preferred_element_type=F32
    ).astype(BF16)

    def contract(e, _):
        part[e] = lax.dot_general(
            window, three[e], (((1,), (1,)), ((), ())), preferred_element_type=F32
        )
        return 0

    lax.fori_loop(0, count, contract, 0, unroll=4)

    def first_block(d):
        return (d * slab) // lanes

    def piece(d, c, j):
        return part[tab_ref[c, first_block(d) + j], 16 * c : 16 * (c + 1), :]

    def c_copy(t):
        return pltpu.make_async_remote_copy(
            src_ref=csend.at[t], dst_ref=crecv.at[t],
            send_sem=cs_sems.at[t], recv_sem=cr_sems.at[t],
            device_id=(other, p), device_id_type=MESH,
        )

    def d_copy(t, slot):
        return pltpu.make_async_remote_copy(
            src_ref=dsend.at[t], dst_ref=drecv.at[slot],
            send_sem=ds_sems.at[t], recv_sem=dr_sems.at[slot],
            device_id=(2 * t + core, p), device_id_type=MESH,
        )

    def to_core(s, _):
        t = (my_t + s) % n_t
        d = 2 * t + 1 - core
        for c in range(2):
            for j in range(nb):
                csend[t, 16 * c : 16 * (c + 1), lanes * j : lanes * (j + 1)] = piece(d, c, j)
        c_copy(t).start()
        return 0

    lax.fori_loop(1, n_t + 1, to_core, 0)

    def to_chip(s, _):
        t = (my_t + s) % n_t
        d = 2 * t + core
        c_copy(t).wait_recv()
        for c in range(2):
            for j in range(nb):
                here = (slice(16 * c, 16 * (c + 1)), slice(lanes * j, lanes * (j + 1)))
                dsend[(t,) + here] = (piece(d, c, j) + crecv[(t,) + here]).astype(BF16)
        d_copy(t, my_t).start()
        return 0

    lax.fori_loop(1, n_t, to_chip, 0)
    c_copy(my_t).wait_recv()

    for load in loads[3:]:
        load.wait()
    first_energy = occ_ref[pair_ref[p // 2, 0]]
    second_energy = occ_ref[pair_ref[p // 2, 1]]
    first = first_block(me)
    offset = me * slab - first * lanes
    sub = lax.broadcasted_iota(jnp.int32, (16, lanes), 0)
    lane = lax.broadcasted_iota(jnp.int32, (16, lanes), 1)
    tops = jnp.where(sub < HALF, ven_ref[0:1, :], ven_ref[nvb : nvb + 1, :])
    column = jnp.sum(jnp.where(lane == sub % HALF, tops, 0.0), axis=1, keepdims=True)

    totals = []
    for c in range(2):
        for j in range(nb):
            here = (slice(16 * c, 16 * (c + 1)), slice(lanes * j, lanes * (j + 1)))
            totals.append(piece(me, c, j) + crecv[(my_t,) + here])

    def arrive(s, totals):
        t = (my_t + n_t - s) % n_t
        pltpu.make_async_remote_copy(
            src_ref=dsend.at[t], dst_ref=drecv.at[t],
            send_sem=ds_sems.at[t], recv_sem=dr_sems.at[t],
            device_id=(2 * t + core, p), device_id_type=MESH,
        ).wait_recv()
        out = []
        for c in range(2):
            for j in range(nb):
                here = (slice(16 * c, 16 * (c + 1)), slice(lanes * j, lanes * (j + 1)))
                out.append(totals[c * nb + j] + drecv[(t,) + here].astype(F32))
        return tuple(out)

    totals = lax.fori_loop(1, n_t, arrive, tuple(totals))

    grams = [[jnp.zeros((HALF, HALF), F32) for _ in range(2)] for _ in range(2)]
    for j in range(nb):
        energy = ven_ref[pl.ds(half * nvb + first + j, 1), :]
        denominator = column + energy - first_energy - second_energy
        heads, tails = [], []
        for c in range(2):
            scaled = (totals[c * nb + j] / denominator).astype(BF16)
            if c == 0:
                amp_ref[:, lanes * j : lanes * (j + 1)] = scaled
            wide = scaled.astype(F32)
            if slab % lanes:
                at = lane + (j * lanes - offset)
                wide = jnp.where(jnp.logical_and(at >= 0, at < slab), wide, 0.0)
            heads.append(wide[:HALF].astype(BF16))
            tails.append(wide[HALF:].astype(BF16))
        for a in range(2):
            for b in range(2):
                grams[a][b] += lax.dot_general(
                    heads[a], tails[b], (((1,), (1,)), ((), ())), preferred_element_type=F32
                )
    psum_buf[p, :, :HALF] = (
        2.0 * (grams[0][0] + grams[1][1]) - grams[1][0] - grams[0][1]
    )

    def p_copy(q, slot):
        return pltpu.make_async_remote_copy(
            src_ref=psum_buf.at[p], dst_ref=psum_buf.at[slot],
            send_sem=ps_sems.at[q], recv_sem=pr_sems.at[slot],
            device_id=(me, q), device_id_type=MESH,
        )

    def p_send(s, _):
        p_copy((p + s) % n_pair, p).start()
        return 0

    lax.fori_loop(1, n_pair, p_send, 0)

    def p_wait(s, _):
        q = (p + s) % n_pair
        p_copy(q, q).wait()
        return 0

    lax.fori_loop(1, n_pair, p_wait, 0)
    total = psum_buf[0]
    for q in range(1, n_pair):
        total = total + psum_buf[q]
    asum_buf[me] = total

    def a_copy(d, slot):
        return pltpu.make_async_remote_copy(
            src_ref=asum_buf.at[me], dst_ref=asum_buf.at[slot],
            send_sem=as_sems.at[d], recv_sem=ar_sems.at[slot],
            device_id=(d, p), device_id_type=MESH,
        )

    def a_send(s, _):
        a_copy((me + s) % n_aux, me).start()
        return 0

    lax.fori_loop(1, n_aux, a_send, 0)

    def sent(s, _):
        t = (my_t + s) % n_t
        d_copy(t, my_t).wait_send()
        c_copy(t).wait_send()
        return 0

    lax.fori_loop(1, n_t, sent, 0)
    c_copy(my_t).wait_send()

    def a_wait(s, _):
        d = (me + s) % n_aux
        a_copy(d, d).wait()
        return 0

    lax.fori_loop(1, n_aux, a_wait, 0)
    total = asum_buf[0]
    for d in range(1, n_aux):
        total = total + asum_buf[d]
    den_ref[...] = (total / math.sqrt(V))[:, :HALF]


def body(blocks, block_list, metric, virt_energy, occ_energy, pair_list):
    n_aux = lax.axis_size("aux")
    n_pair = lax.axis_size("pair")
    raw = blocks[0, 0]
    entries = jnp.transpose(block_list[0], (2, 0, 1))
    count, lanes = raw.shape[0], raw.shape[1]
    width = virt_energy.shape[0] // 2
    nvb = width // lanes
    slab = width // n_aux
    nb = max(-(-((d + 1) * slab) // lanes) - d * slab // lanes for d in range(n_aux))
    shard = metric.shape[1]
    n_t = n_aux // 2
    vmem = pl.BlockSpec(memory_space=pltpu.VMEM)
    hbm = pl.BlockSpec(memory_space=pltpu.HBM)
    dma = pltpu.SemaphoreType.DMA
    amp, density = pl.pallas_call(
        functools.partial(main_kernel, n_aux, n_pair, nvb, slab, nb),
        out_shape=(
            jax.ShapeDtypeStruct((2 * HALF, nb * lanes), BF16),
            jax.ShapeDtypeStruct((HALF, HALF), F32),
        ),
        in_specs=[hbm] * 6,
        out_specs=(vmem, vmem),
        scratch_shapes=[
            pltpu.SMEM((3, 1, count), jnp.int32),
            pltpu.SMEM(occ_energy.shape, F32),
            pltpu.SMEM(pair_list.shape, jnp.int32),
            pltpu.VMEM(metric.shape, BF16),
            pltpu.VMEM((2 * nvb, lanes), F32),
            pltpu.VMEM((8, 128), jnp.int32),
            pltpu.SMEM((8, 128), jnp.int32),
            pltpu.VMEM((count + 1, lanes, raw.shape[2]), BF16),
            pltpu.VMEM((count, lanes, shard), BF16),
            pltpu.VMEM((count + 1, 32, lanes), F32),
            pltpu.VMEM((32, lanes), BF16),
            pltpu.VMEM((32, lanes), BF16),
            pltpu.VMEM((n_t, 32, nb * lanes), F32),
            pltpu.VMEM((n_t, 32, nb * lanes), F32),
            pltpu.VMEM((n_t, 32, nb * lanes), BF16),
            pltpu.VMEM((n_t, 32, nb * lanes), BF16),
            pltpu.VMEM((n_pair, HALF, lanes), F32),
            pltpu.VMEM((n_aux, HALF, lanes), F32),
            dma((7,)),
            dma((2,)),
            dma((n_t,)),
            dma((n_t,)),
            dma((n_t,)),
            dma((n_t,)),
            dma((n_pair,)),
            dma((n_pair,)),
            dma((n_aux,)),
            dma((n_aux,)),
        ],
        compiler_params=pltpu.CompilerParams(
            collective_id=0, has_side_effects=True, vmem_limit_bytes=60 * 2**20
        ),
        name="amplitudes",
    )(entries, occ_energy, pair_list, raw, metric, virt_energy.reshape(-1, lanes))
    if slab % lanes:
        me = lax.axis_index("aux")
        amp = lax.dynamic_slice_in_dim(amp, me * slab - me * slab // lanes * lanes, slab, 1)
    return (amp[None], density)


def solution(mesh):
    in_specs = (
        P("aux", "pair", None, None, None),
        P("aux", "pair", None, None),
        P("aux", None),
        P(),
        P(),
        P(),
    )
    out_specs = (P("pair", None, "aux"), P())
    return jax.shard_map(body, mesh=mesh, in_specs=in_specs, out_specs=out_specs, check_vma=False)
```

```python
import functools
import math

import jax
import jax.numpy as jnp
from jax import lax
from jax.experimental import pallas as pl
from jax.experimental.pallas import tpu as pltpu
from jax.sharding import PartitionSpec as P

V = 20480
HALF = 8
MESH = pl.DeviceIdType.MESH
F32 = jnp.float32
BF16 = jnp.bfloat16


def wrap(i, n):
    return jnp.where(i >= n, i - n, i)


def index_table(nvb, count, list_ref):
    row = lax.broadcasted_iota(jnp.int32, (8, 128), 0)
    lane = lax.broadcasted_iota(jnp.int32, (8, 128), 1)

    def slot_of(e):
        o = list_ref[0, 0, e]
        return jnp.where(o >= 0, o * nvb + list_ref[1, 0, e], -1)

    def spread(e, slots):
        return jnp.where(lane == e, slot_of(e), slots)

    slots = lax.fori_loop(0, count, spread, jnp.full((8, 128), -2, jnp.int32), unroll=8)
    slots = jnp.where(slots < 0, -2, slots)
    by_block = jnp.where(lane < nvb, jnp.where(row == 0, nvb + lane, lane), -2)
    by_window = jnp.where(lane < 4, jnp.where(lane < 2, 0, nvb), -2)
    key = jnp.where(row < 2, by_block, jnp.where(row < 4, slots, by_window))
    aux = jnp.where(row < 2, -1, jnp.where(row < 4, row - 2, jnp.bitwise_and(lane, 1)))

    def enter(e, table):
        hit = (key == slot_of(e)) & ((aux < 0) | (aux == list_ref[2, 0, e]))
        return jnp.where(hit, e, table)

    return lax.fori_loop(0, count, enter, jnp.full((8, 128), count, jnp.int32), unroll=8)


def main_kernel(
    n_aux, n_pair, nvb, slab, nb,
    list_hbm, occ_hbm, pair_hbm, blocks_ref, metric_hbm, ven_hbm,
    amp_ref, den_ref,
    list_ref, occ_ref, pair_ref, metric_ref, ven_ref, tab_vmem, tab_ref,
    held, three, part, wsend, wrecv, csend, crecv, xsend, xrecv, zsend, zrecv, sums,
    load_sems, w_sems, cs_sems, cr_sems, xs_sems, xr_sems, zs_sems, zr_sems, sum_sems,
):
    count = blocks_ref.shape[0]
    lanes = blocks_ref.shape[1]
    n_t = n_aux // 2
    me = lax.axis_index("aux")
    p = lax.axis_index("pair")
    core = me % 2
    my_t = me // 2
    n_u = n_t // 2
    side = my_t % 2
    my_u = my_t // 2
    half = p % 2
    mate = p + 1 - 2 * half
    other = me + 1 - 2 * core

    loads = [
        pltpu.make_async_copy(src, dst, load_sems.at[i])
        for i, (src, dst) in enumerate([
            (list_hbm, list_ref),
            (blocks_ref, held.at[pl.ds(0, count)]),
            (metric_hbm, metric_ref),
            (pair_hbm, pair_ref),
            (occ_hbm, occ_ref),
            (ven_hbm, ven_ref),
        ])
    ]
    for load in loads:
        load.start()

    barrier = pltpu.get_barrier_semaphore()

    def greet(s, _):
        for q in range(n_pair):
            @pl.when((s > 0) | (q > 0))
            def _():
                pl.semaphore_signal(
                    barrier, inc=1, device_id=(wrap(me + s, n_aux), wrap(p + q, n_pair)),
                    device_id_type=MESH,
                )
        return 0

    lax.fori_loop(0, n_aux, greet, 0, unroll=8)

    held[count] = jnp.zeros(held.shape[1:], BF16)
    part[count] = jnp.zeros(part.shape[1:], F32)
    loads[0].wait()
    tab_vmem[...] = index_table(nvb, count, list_ref)
    fill = pltpu.make_async_copy(tab_vmem, tab_ref, load_sems.at[len(loads)])
    fill.start()
    loads[1].wait()
    fill.wait()
    own = [held[tab_ref[4, i], :16, :].astype(F32)[:HALF] for i in range(4)]
    wsend[...] = jnp.concatenate(own, axis=0).astype(BF16)
    pl.semaphore_wait(barrier, n_aux * n_pair - 1)
    wcopy = pltpu.make_async_remote_copy(
        src_ref=wsend, dst_ref=wrecv, send_sem=w_sems.at[0], recv_sem=w_sems.at[1],
        device_id=(me, mate), device_id_type=MESH,
    )
    wcopy.start()

    loads[2].wait()
    metric = metric_ref[...]

    def transform(e, _):
        rows = jnp.concatenate(
            [held[tab_ref[2, e]], held[tab_ref[3, e]]], axis=1
        )
        three[e] = jnp.dot(rows, metric, preferred_element_type=F32).astype(BF16)
        return 0

    lax.fori_loop(0, count, transform, 0, unroll=4)

    wcopy.wait()
    theirs = wrecv[...].astype(F32)
    rows = []
    for o in range(2):
        mine = jnp.concatenate([own[2 * o], own[2 * o + 1]], axis=1)
        got = jnp.concatenate(
            [theirs[16 * o : 16 * o + HALF], theirs[16 * o + HALF : 16 * o + 16]], axis=1
        )
        rows.append(jnp.where(half == 0, mine, got))
        rows.append(jnp.where(half == 0, got, mine))
    window = jnp.dot(
        jnp.concatenate(rows, axis=0).astype(BF16), metric, preferred_element_type=F32
    ).astype(BF16)

    def contract(e, _):
        part[e] = lax.dot_general(
            window, three[e], (((1,), (1,)), ((), ())), preferred_element_type=F32
        )
        return 0

    lax.fori_loop(0, count, contract, 0, unroll=32)

    def first_block(d):
        return (d * slab) // lanes

    def piece(d, c, j):
        return part[tab_ref[c, first_block(d) + j], 16 * c : 16 * (c + 1), :]

    def c_copy(t):
        return pltpu.make_async_remote_copy(
            src_ref=csend.at[t], dst_ref=crecv.at[t],
            send_sem=cs_sems.at[t], recv_sem=cr_sems.at[t],
            device_id=(other, p), device_id_type=MESH,
        )

    def x_copy(u):
        return pltpu.make_async_remote_copy(
            src_ref=xsend.at[u], dst_ref=xrecv.at[u],
            send_sem=xs_sems.at[u], recv_sem=xr_sems.at[u],
            device_id=(2 * (my_t + 1 - 2 * side) + core, p), device_id_type=MESH,
        )

    def z_copy(u, slot):
        return pltpu.make_async_remote_copy(
            src_ref=zsend.at[u], dst_ref=zrecv.at[slot],
            send_sem=zs_sems.at[u], recv_sem=zr_sems.at[slot],
            device_id=(2 * (2 * u + side) + core, p), device_id_type=MESH,
        )

    def turn(i):
        split = n_u - n_u // 2
        step = jnp.where(i < split, n_u // 2 + i, i - split + 1)
        return wrap(my_u + jnp.where(i == n_u - 1, 0, step), n_u)

    tiles = [
        (c, j, (slice(16 * c, 16 * (c + 1)), slice(lanes * j, lanes * (j + 1))))
        for c in range(2)
        for j in range(nb)
    ]

    def to_core(i, _):
        u = turn(i)
        for b in (1 - side, side):
            t = 2 * u + b
            for c, j, here in tiles:
                csend[(t,) + here] = piece(2 * t + 1 - core, c, j)
            c_copy(t).start()
        return 0

    lax.fori_loop(0, n_u, to_core, 0)

    def to_side(i, _):
        u = turn(i)
        t = 2 * u + 1 - side
        c_copy(t).wait_recv()
        for c, j, here in tiles:
            xsend[(u,) + here] = (piece(2 * t + core, c, j) + crecv[(t,) + here]).astype(BF16)
        x_copy(u).start()
        return 0

    lax.fori_loop(0, n_u, to_side, 0)

    def merged(u, c, j, here):
        t = 2 * u + side
        return piece(2 * t + core, c, j) + crecv[(t,) + here] + xrecv[(u,) + here].astype(F32)

    def to_line(i, _):
        u = turn(i)
        c_copy(2 * u + side).wait_recv()
        x_copy(u).wait_recv()
        for c, j, here in tiles:
            zsend[(u,) + here] = merged(u, c, j, here).astype(BF16)
        z_copy(u, my_u).start()
        return 0

    lax.fori_loop(0, n_u - 1, to_line, 0)

    for load in loads[3:]:
        load.wait()
    first_energy = occ_ref[pair_ref[p // 2, 0]]
    second_energy = occ_ref[pair_ref[p // 2, 1]]
    first = first_block(me)
    offset = me * slab - first * lanes
    sub = lax.broadcasted_iota(jnp.int32, (16, lanes), 0)
    lane = lax.broadcasted_iota(jnp.int32, (16, lanes), 1)
    tops = jnp.where(sub < HALF, ven_ref[0:1, :], ven_ref[nvb : nvb + 1, :])
    column = jnp.sum(jnp.where(lane == sub % HALF, tops, 0.0), axis=1, keepdims=True)

    c_copy(my_t).wait_recv()
    x_copy(my_u).wait_recv()
    totals = [merged(my_u, c, j, here) for c, j, here in tiles]

    def arrive(s, totals):
        u = wrap(my_u + s, n_u)
        z_copy(u, u).wait_recv()
        return tuple(
            total + zrecv[(u,) + here].astype(F32)
            for total, (_, _, here) in zip(totals, tiles)
        )

    totals = lax.fori_loop(1, n_u, arrive, tuple(totals))

    grams = [[jnp.zeros((HALF, HALF), F32) for _ in range(2)] for _ in range(2)]
    for j in range(nb):
        energy = ven_ref[pl.ds(half * nvb + first + j, 1), :]
        denominator = column + energy - first_energy - second_energy
        heads, tails = [], []
        for c in range(2):
            scaled = (totals[c * nb + j] / denominator).astype(BF16)
            if c == 0:
                amp_ref[:, lanes * j : lanes * (j + 1)] = scaled
            wide = scaled.astype(F32)
            if slab % lanes:
                at = lane + (j * lanes - offset)
                wide = jnp.where(jnp.logical_and(at >= 0, at < slab), wide, 0.0)
            heads.append(wide[:HALF].astype(BF16))
            tails.append(wide[HALF:].astype(BF16))
        for a in range(2):
            for b in range(2):
                grams[a][b] += lax.dot_general(
                    heads[a], tails[b], (((1,), (1,)), ((), ())), preferred_element_type=F32
                )
    mine = me * n_pair + p
    sums[mine] = jnp.zeros(sums.shape[1:], F32)
    sums[mine, :, :HALF] = 2.0 * (grams[0][0] + grams[1][1]) - grams[1][0] - grams[0][1]

    def share(s, _):
        for q in range(n_pair):
            @pl.when((s > 0) | (q > 0))
            def _():
                pltpu.make_async_remote_copy(
                    src_ref=sums.at[mine], dst_ref=sums.at[mine],
                    send_sem=sum_sems.at[0], recv_sem=sum_sems.at[1],
                    device_id=(wrap(me + s, n_aux), wrap(p + q, n_pair)), device_id_type=MESH,
                ).start()
        return 0

    lax.fori_loop(0, n_aux, share, 0, unroll=8)

    def sent(u, _):
        c_copy(2 * u).wait_send()
        c_copy(2 * u + 1).wait_send()
        x_copy(u).wait_send()
        pl.when(u != my_u)(lambda: z_copy(u, my_u).wait_send())
        return 0

    lax.fori_loop(0, n_u, sent, 0)
    peers = sums.at[pl.ds(0, n_aux * n_pair - 1)]
    pltpu.make_async_copy(peers, peers, sum_sems.at[0]).wait()
    pltpu.make_async_copy(peers, peers, sum_sems.at[1]).wait()
    total = sums[0]
    for d in range(1, n_aux * n_pair):
        total = total + sums[d]
    den_ref[...] = (total / math.sqrt(V))[:, :HALF]


def body(blocks, block_list, metric, virt_energy, occ_energy, pair_list):
    n_aux = lax.axis_size("aux")
    n_pair = lax.axis_size("pair")
    raw = blocks[0, 0]
    entries = jnp.transpose(block_list[0], (2, 0, 1))
    count, lanes = raw.shape[0], raw.shape[1]
    width = virt_energy.shape[0] // 2
    nvb = width // lanes
    slab = width // n_aux
    nb = max(-(-((d + 1) * slab) // lanes) - d * slab // lanes for d in range(n_aux))
    shard = metric.shape[1]
    n_t = n_aux // 2
    n_u = n_t // 2
    vmem = pl.BlockSpec(memory_space=pltpu.VMEM)
    hbm = pl.BlockSpec(memory_space=pltpu.HBM)
    dma = pltpu.SemaphoreType.DMA
    amp, density = pl.pallas_call(
        functools.partial(main_kernel, n_aux, n_pair, nvb, slab, nb),
        out_shape=(
            jax.ShapeDtypeStruct((2 * HALF, nb * lanes), BF16),
            jax.ShapeDtypeStruct((HALF, HALF), F32),
        ),
        in_specs=[hbm] * 6,
        out_specs=(vmem, vmem),
        scratch_shapes=[
            pltpu.SMEM((3, 1, count), jnp.int32),
            pltpu.SMEM(occ_energy.shape, F32),
            pltpu.SMEM(pair_list.shape, jnp.int32),
            pltpu.VMEM(metric.shape, BF16),
            pltpu.VMEM((2 * nvb, lanes), F32),
            pltpu.VMEM((8, 128), jnp.int32),
            pltpu.SMEM((8, 128), jnp.int32),
            pltpu.VMEM((count + 1, lanes, raw.shape[2]), BF16),
            pltpu.VMEM((count, lanes, shard), BF16),
            pltpu.VMEM((count + 1, 32, lanes), F32),
            pltpu.VMEM((32, lanes), BF16),
            pltpu.VMEM((32, lanes), BF16),
            pltpu.VMEM((n_t, 32, nb * lanes), F32),
            pltpu.VMEM((n_t, 32, nb * lanes), F32),
            pltpu.VMEM((n_u, 32, nb * lanes), BF16),
            pltpu.VMEM((n_u, 32, nb * lanes), BF16),
            pltpu.VMEM((n_u, 32, nb * lanes), BF16),
            pltpu.VMEM((n_u, 32, nb * lanes), BF16),
            pltpu.VMEM((n_aux * n_pair, HALF, lanes), F32),
            dma((7,)),
            dma((2,)),
            dma((n_t,)),
            dma((n_t,)),
            dma((n_u,)),
            dma((n_u,)),
            dma((n_u,)),
            dma((n_u,)),
            dma((2,)),
        ],
        compiler_params=pltpu.CompilerParams(
            collective_id=0, has_side_effects=True, vmem_limit_bytes=60 * 2**20
        ),
        name="amplitudes",
    )(entries, occ_energy, pair_list, raw, metric, virt_energy.reshape(-1, lanes))
    if slab % lanes:
        me = lax.axis_index("aux")
        amp = lax.dynamic_slice_in_dim(amp, me * slab - me * slab // lanes * lanes, slab, 1)
    return (amp[None], density)


def solution(mesh):
    in_specs = (
        P("aux", "pair", None, None, None),
        P("aux", "pair", None, None),
        P("aux", None),
        P(),
        P(),
        P(),
    )
    out_specs = (P("pair", None, "aux"), P())
    return jax.shard_map(body, mesh=mesh, in_specs=in_specs, out_specs=out_specs, check_vma=False)
```

```python
import functools
import math

import jax
import jax.numpy as jnp
from jax import lax
from jax.experimental import pallas as pl
from jax.experimental.pallas import tpu as pltpu
from jax.sharding import PartitionSpec as P

V = 20480
HALF = 8
MESH = pl.DeviceIdType.MESH
F32 = jnp.float32
BF16 = jnp.bfloat16


def wrap(i, n):
    return jnp.where(i >= n, i - n, i)


def index_table(nvb, count, list_ref):
    row = lax.broadcasted_iota(jnp.int32, (8, 128), 0)
    lane = lax.broadcasted_iota(jnp.int32, (8, 128), 1)

    def slot_of(e):
        o = list_ref[0, 0, e]
        return jnp.where(o >= 0, o * nvb + list_ref[1, 0, e], -1)

    def spread(e, slots):
        return jnp.where(lane == e, slot_of(e), slots)

    slots = lax.fori_loop(0, count, spread, jnp.full((8, 128), -2, jnp.int32), unroll=8)
    slots = jnp.where(slots < 0, -2, slots)
    by_block = jnp.where(lane < nvb, jnp.where(row == 0, nvb + lane, lane), -2)
    by_window = jnp.where(lane < 4, jnp.where(lane < 2, 0, nvb), -2)
    key = jnp.where(row < 2, by_block, jnp.where(row < 4, slots, by_window))
    aux = jnp.where(row < 2, -1, jnp.where(row < 4, row - 2, jnp.bitwise_and(lane, 1)))

    def enter(e, table):
        hit = (key == slot_of(e)) & ((aux < 0) | (aux == list_ref[2, 0, e]))
        return jnp.where(hit, e, table)

    return lax.fori_loop(0, count, enter, jnp.full((8, 128), count, jnp.int32), unroll=8)


def main_kernel(
    n_aux, n_pair, nvb, slab, nb,
    list_hbm, occ_hbm, pair_hbm, blocks_ref, metric_hbm, ven_hbm,
    amp_ref, den_ref,
    list_ref, occ_ref, pair_ref, metric_ref, ven_ref, tab_vmem, tab_ref,
    held, three, part, wsend, wrecv, csend, crecv, xsend, xrecv, zsend, zrecv, sums,
    load_sems, w_sems, cs_sems, cr_sems, xs_sems, xr_sems, zs_sems, zr_sems, sum_sems,
):
    count = blocks_ref.shape[0]
    lanes = blocks_ref.shape[1]
    n_t = n_aux // 2
    me = lax.axis_index("aux")
    p = lax.axis_index("pair")
    core = me % 2
    my_t = me // 2
    n_u = n_t // 2
    side = my_t % 2
    my_u = my_t // 2
    half = p % 2
    mate = p + 1 - 2 * half
    other = me + 1 - 2 * core

    loads = [
        pltpu.make_async_copy(src, dst, load_sems.at[i])
        for i, (src, dst) in enumerate([
            (list_hbm, list_ref),
            (blocks_ref, held.at[pl.ds(0, count)]),
            (metric_hbm, metric_ref),
            (pair_hbm, pair_ref),
            (occ_hbm, occ_ref),
            (ven_hbm, ven_ref),
        ])
    ]
    for load in loads:
        load.start()

    sums[me * n_pair + p] = jnp.zeros(sums.shape[1:], F32)
    barrier = pltpu.get_barrier_semaphore()

    def greet(s, q):
        pl.semaphore_signal(
            barrier, inc=1, device_id=(wrap(me + s, n_aux), wrap(p + q, n_pair)),
            device_id_type=MESH,
        )

    def greet_all(s, _):
        for q in range(n_pair):
            greet(s, q)
        return 0

    for q in range(1, n_pair):
        greet(0, q)
    lax.fori_loop(1, n_aux, greet_all, 0, unroll=5)

    held[count] = jnp.zeros(held.shape[1:], BF16)
    part[count] = jnp.zeros(part.shape[1:], F32)
    loads[0].wait()
    tab_vmem[...] = index_table(nvb, count, list_ref)
    fill = pltpu.make_async_copy(tab_vmem, tab_ref, load_sems.at[len(loads)])
    fill.start()
    loads[1].wait()
    fill.wait()
    own = [held[tab_ref[4, i], :16, :].astype(F32)[:HALF] for i in range(4)]
    wsend[...] = jnp.concatenate(own, axis=0).astype(BF16)
    pl.semaphore_wait(barrier, n_aux * n_pair - 1)
    wcopy = pltpu.make_async_remote_copy(
        src_ref=wsend, dst_ref=wrecv, send_sem=w_sems.at[0], recv_sem=w_sems.at[1],
        device_id=(me, mate), device_id_type=MESH,
    )
    wcopy.start()

    loads[2].wait()
    metric = metric_ref[...]

    def transform(e, _):
        rows = jnp.concatenate(
            [held[tab_ref[2, e]], held[tab_ref[3, e]]], axis=1
        )
        three[e] = jnp.dot(rows, metric, preferred_element_type=F32).astype(BF16)
        return 0

    lax.fori_loop(0, count, transform, 0, unroll=4)

    wcopy.wait()
    theirs = wrecv[...].astype(F32)
    rows = []
    for o in range(2):
        mine = jnp.concatenate([own[2 * o], own[2 * o + 1]], axis=1)
        got = jnp.concatenate(
            [theirs[16 * o : 16 * o + HALF], theirs[16 * o + HALF : 16 * o + 16]], axis=1
        )
        rows.append(jnp.where(half == 0, mine, got))
        rows.append(jnp.where(half == 0, got, mine))
    window = jnp.dot(
        jnp.concatenate(rows, axis=0).astype(BF16), metric, preferred_element_type=F32
    ).astype(BF16)

    def contract(e, _):
        part[e] = lax.dot_general(
            window, three[e], (((1,), (1,)), ((), ())), preferred_element_type=F32
        )
        return 0

    lax.fori_loop(0, count, contract, 0, unroll=32)

    def first_block(d):
        return (d * slab) // lanes

    def piece(d, c, j):
        return part[tab_ref[c, first_block(d) + j], 16 * c : 16 * (c + 1), :]

    def c_copy(t):
        return pltpu.make_async_remote_copy(
            src_ref=csend.at[t], dst_ref=crecv.at[t],
            send_sem=cs_sems.at[t], recv_sem=cr_sems.at[t],
            device_id=(other, p), device_id_type=MESH,
        )

    def x_copy(u):
        return pltpu.make_async_remote_copy(
            src_ref=xsend.at[u], dst_ref=xrecv.at[u],
            send_sem=xs_sems.at[u], recv_sem=xr_sems.at[u],
            device_id=(2 * (my_t + 1 - 2 * side) + core, p), device_id_type=MESH,
        )

    def z_copy(u, slot):
        return pltpu.make_async_remote_copy(
            src_ref=zsend.at[u], dst_ref=zrecv.at[slot],
            send_sem=zs_sems.at[u], recv_sem=zr_sems.at[slot],
            device_id=(2 * (2 * u + side) + core, p), device_id_type=MESH,
        )

    def turn(i):
        split = n_u - n_u // 2
        step = jnp.where(i < split, n_u // 2 + i, i - split + 1)
        return wrap(my_u + jnp.where(i == n_u - 1, 0, step), n_u)

    tiles = [
        (c, j, (slice(16 * c, 16 * (c + 1)), slice(lanes * j, lanes * (j + 1))))
        for c in range(2)
        for j in range(nb)
    ]

    def to_core(i, _):
        u = turn(i)
        for b in (1 - side, side):
            t = 2 * u + b
            for c, j, here in tiles:
                csend[(t,) + here] = piece(2 * t + 1 - core, c, j)
            c_copy(t).start()
        return 0

    lax.fori_loop(0, n_u, to_core, 0)

    def to_side(i, _):
        u = turn(i)
        t = 2 * u + 1 - side
        c_copy(t).wait_recv()
        for c, j, here in tiles:
            xsend[(u,) + here] = (piece(2 * t + core, c, j) + crecv[(t,) + here]).astype(BF16)
        x_copy(u).start()
        return 0

    lax.fori_loop(0, n_u, to_side, 0)

    def merged(u, c, j, here):
        t = 2 * u + side
        return piece(2 * t + core, c, j) + crecv[(t,) + here] + xrecv[(u,) + here].astype(F32)

    def to_line(i, _):
        u = turn(i)
        c_copy(2 * u + side).wait_recv()
        x_copy(u).wait_recv()
        for c, j, here in tiles:
            zsend[(u,) + here] = merged(u, c, j, here).astype(BF16)
        z_copy(u, my_u).start()
        return 0

    lax.fori_loop(0, n_u - 1, to_line, 0)

    for load in loads[3:]:
        load.wait()
    first_energy = occ_ref[pair_ref[p // 2, 0]]
    second_energy = occ_ref[pair_ref[p // 2, 1]]
    first = first_block(me)
    offset = me * slab - first * lanes
    sub = lax.broadcasted_iota(jnp.int32, (16, lanes), 0)
    lane = lax.broadcasted_iota(jnp.int32, (16, lanes), 1)
    tops = jnp.where(sub < HALF, ven_ref[0:1, :], ven_ref[nvb : nvb + 1, :])
    column = jnp.sum(jnp.where(lane == sub % HALF, tops, 0.0), axis=1, keepdims=True)

    c_copy(my_t).wait_recv()
    x_copy(my_u).wait_recv()
    totals = [merged(my_u, c, j, here) for c, j, here in tiles]

    def arrive(s, totals):
        u = wrap(my_u + s, n_u)
        z_copy(u, u).wait_recv()
        return tuple(
            total + zrecv[(u,) + here].astype(F32)
            for total, (_, _, here) in zip(totals, tiles)
        )

    totals = lax.fori_loop(1, n_u, arrive, tuple(totals))

    grams = [[jnp.zeros((HALF, HALF), F32) for _ in range(2)] for _ in range(2)]
    for j in range(nb):
        energy = ven_ref[pl.ds(half * nvb + first + j, 1), :]
        denominator = column + energy - first_energy - second_energy
        heads, tails = [], []
        for c in range(2):
            scaled = (totals[c * nb + j] / denominator).astype(BF16)
            if c == 0:
                amp_ref[:, lanes * j : lanes * (j + 1)] = scaled
            wide = scaled.astype(F32)
            if slab % lanes:
                at = lane + (j * lanes - offset)
                wide = jnp.where(jnp.logical_and(at >= 0, at < slab), wide, 0.0)
            heads.append(wide[:HALF].astype(BF16))
            tails.append(wide[HALF:].astype(BF16))
        for a in range(2):
            for b in range(2):
                grams[a][b] += lax.dot_general(
                    heads[a], tails[b], (((1,), (1,)), ((), ())), preferred_element_type=F32
                )
    mine = me * n_pair + p
    sums[mine, :, :HALF] = 2.0 * (grams[0][0] + grams[1][1]) - grams[1][0] - grams[0][1]

    def share(s, q):
        pltpu.make_async_remote_copy(
            src_ref=sums.at[mine], dst_ref=sums.at[mine],
            send_sem=sum_sems.at[0], recv_sem=sum_sems.at[1],
            device_id=(wrap(me + s, n_aux), wrap(p + q, n_pair)), device_id_type=MESH,
        ).start()

    def share_all(s, _):
        for q in range(n_pair):
            share(s, q)
        return 0

    lax.fori_loop(1, n_aux, share_all, 0, unroll=5)
    for q in range(1, n_pair):
        share(0, q)

    def sent(u, _):
        c_copy(2 * u).wait_send()
        c_copy(2 * u + 1).wait_send()
        x_copy(u).wait_send()
        pl.when(u != my_u)(lambda: z_copy(u, my_u).wait_send())
        return 0

    lax.fori_loop(0, n_u, sent, 0)
    peers = sums.at[pl.ds(0, n_aux * n_pair - 1)]
    pltpu.make_async_copy(peers, peers, sum_sems.at[0]).wait()
    pltpu.make_async_copy(peers, peers, sum_sems.at[1]).wait()
    total = sums[0]
    for d in range(1, n_aux * n_pair):
        total = total + sums[d]
    den_ref[...] = (total / math.sqrt(V))[:, :HALF]


def body(blocks, block_list, metric, virt_energy, occ_energy, pair_list):
    n_aux = lax.axis_size("aux")
    n_pair = lax.axis_size("pair")
    raw = blocks[0, 0]
    entries = jnp.transpose(block_list[0], (2, 0, 1))
    count, lanes = raw.shape[0], raw.shape[1]
    width = virt_energy.shape[0] // 2
    nvb = width // lanes
    slab = width // n_aux
    nb = max(-(-((d + 1) * slab) // lanes) - d * slab // lanes for d in range(n_aux))
    shard = metric.shape[1]
    n_t = n_aux // 2
    n_u = n_t // 2
    vmem = pl.BlockSpec(memory_space=pltpu.VMEM)
    hbm = pl.BlockSpec(memory_space=pltpu.HBM)
    dma = pltpu.SemaphoreType.DMA
    amp, density = pl.pallas_call(
        functools.partial(main_kernel, n_aux, n_pair, nvb, slab, nb),
        out_shape=(
            jax.ShapeDtypeStruct((2 * HALF, nb * lanes), BF16),
            jax.ShapeDtypeStruct((HALF, HALF), F32),
        ),
        in_specs=[hbm] * 6,
        out_specs=(vmem, vmem),
        scratch_shapes=[
            pltpu.SMEM((3, 1, count), jnp.int32),
            pltpu.SMEM(occ_energy.shape, F32),
            pltpu.SMEM(pair_list.shape, jnp.int32),
            pltpu.VMEM(metric.shape, BF16),
            pltpu.VMEM((2 * nvb, lanes), F32),
            pltpu.VMEM((8, 128), jnp.int32),
            pltpu.SMEM((8, 128), jnp.int32),
            pltpu.VMEM((count + 1, lanes, raw.shape[2]), BF16),
            pltpu.VMEM((count, lanes, shard), BF16),
            pltpu.VMEM((count + 1, 32, lanes), F32),
            pltpu.VMEM((32, lanes), BF16),
            pltpu.VMEM((32, lanes), BF16),
            pltpu.VMEM((n_t, 32, nb * lanes), F32),
            pltpu.VMEM((n_t, 32, nb * lanes), F32),
            pltpu.VMEM((n_u, 32, nb * lanes), BF16),
            pltpu.VMEM((n_u, 32, nb * lanes), BF16),
            pltpu.VMEM((n_u, 32, nb * lanes), BF16),
            pltpu.VMEM((n_u, 32, nb * lanes), BF16),
            pltpu.VMEM((n_aux * n_pair, HALF, lanes), F32),
            dma((7,)),
            dma((2,)),
            dma((n_t,)),
            dma((n_t,)),
            dma((n_u,)),
            dma((n_u,)),
            dma((n_u,)),
            dma((n_u,)),
            dma((2,)),
        ],
        compiler_params=pltpu.CompilerParams(
            collective_id=0, has_side_effects=True, vmem_limit_bytes=60 * 2**20
        ),
        name="amplitudes",
    )(entries, occ_energy, pair_list, raw, metric, virt_energy.reshape(-1, lanes))
    if slab % lanes:
        me = lax.axis_index("aux")
        amp = lax.dynamic_slice_in_dim(amp, me * slab - me * slab // lanes * lanes, slab, 1)
    return (amp[None], density)


def solution(mesh):
    in_specs = (
        P("aux", "pair", None, None, None),
        P("aux", "pair", None, None),
        P("aux", None),
        P(),
        P(),
        P(),
    )
    out_specs = (P("pair", None, "aux"), P())
    return jax.shard_map(body, mesh=mesh, in_specs=in_specs, out_specs=out_specs, check_vma=False)
```
